128 devices in a mesh: dom: 128 (over y, z, x, core).
Axes of the slice: x: 4, y: 4, z: 4, core: 2. Of those that a mesh axis runs over, the one named last changes fastest.
Arguments:
- dofs: float32 [9, 35, 49152], P(None, None, 'dom'), may hold values from -6 to 6
- star: float32 [3, 9, 9, 49152], P(None, None, None, 'dom'), may hold values from -0.6 to 0.6
- flux_minus: float32 [4, 9, 9, 49152], P(None, None, None, 'dom'), may hold values from -0.6 to 0.6
- flux_plus: float32 [4, 9, 9, 49152], P(None, None, None, 'dom'), may hold values from -0.6 to 0.6
- cluster: int32 [49152], P('dom'), may hold values from 0 to 2, as said below
- neighbour: int32 [4, 49152], P(None, 'dom'), may hold values from 0 to 639, as said below
- face_code: int32 [4, 49152], P(None, 'dom'), may hold values from 0 to 11
- send_list: int32 [8, 4096], P(None, 'dom'), may hold values from 0 to 383
- stiffness: float32 [3, 35, 35], replicated, may hold values from -1 to 1
- face_proj: float32 [4, 15, 35], replicated, may hold values from -1 to 1
- face_lift: float32 [4, 35, 15], replicated, may hold values from -1.5 to 1.5
- face_turn: float32 [3, 15, 15], replicated, may hold values from -1.5 to 1.5
Outputs:
- new_dofs: float32 [9, 35, 49152], P(None, None, 'dom')
The draws below stay inside these ranges and needn't reach their ends.
Inputs may be any that keep to these rules, and one draw needn't show every extreme that they name: `cluster`: every partition holds at most 128 fast elements, and one partition holds exactly 128. `neighbour`: A ghost slot never names a partition outside 0 .. 128 - 1.
All inputs are finite; a program needn't handle non-finite values.
Results may differ from the reference program's by a relative error of at most 0.0003.
Values sent between devices are 32-bit elements; how exact they have to be, the bound alone decides.
No kernel may reach another device: no remote copies, remote signals or barrier semaphores. Data moves between devices by JAX's collectives and lax.ppermute only.
A program may use at most 256 MiB of HBM per device.

```python
import math
import jax
import jax.numpy as jnp
from jax import lax

BASIS = 35
QUANT = 9
FACE_BASIS = 15
ORDER = 5
RADIUS = 4
E_DEV = 384
FAST_CAP = 128
SEND = 32
ELEMS = 49152
SENDS = 4096


def draw_cluster(key, part):
    key = jax.random.fold_in(key, 5)
    partitions = ELEMS // E_DEV
    keys = jax.random.split(key, 4)
    fast = jax.random.randint(keys[0], (partitions,), FAST_CAP // 8, FAST_CAP // 2 + 1, dtype=jnp.int32)
    busiest = jax.random.randint(keys[1], (), 0, partitions, dtype=jnp.int32)
    fast = jnp.where(jnp.arange(partitions, dtype=jnp.int32) == busiest, FAST_CAP, fast)
    medium = jax.random.randint(keys[2], (partitions,), E_DEV // 4, E_DEV // 2 + 1, dtype=jnp.int32)

    def shuffle(subkey):
        return jax.random.permutation(subkey, E_DEV).astype(jnp.int32)
    ranks = jax.vmap(shuffle)(jax.random.split(keys[3], partitions))
    kinds = jnp.where(ranks < fast[:, None], 0, jnp.where(ranks < (fast + medium)[:, None], 1, 2))
    return kinds.reshape(ELEMS).astype(jnp.int32)


def draw_neighbour(key, part):
    key = jax.random.fold_in(key, 11)
    partitions = ELEMS // E_DEV
    ghost_count = 2 * RADIUS * SEND
    entries = jax.random.randint(key, (4, ELEMS), 0, E_DEV + ghost_count, dtype=jnp.int32)
    device = (jnp.arange(ELEMS, dtype=jnp.int32) // E_DEV)[None, :]
    which = jnp.maximum(entries - E_DEV, 0) // SEND
    offset = jnp.where(which < RADIUS, which - RADIUS, which - RADIUS + 1)
    source = device - offset
    broken = (entries >= E_DEV) & ((source < 0) | (source >= partitions))
    entries = jnp.where(broken, entries % E_DEV, entries)
    entries = entries.at[0, RADIUS * E_DEV].set(E_DEV + ghost_count - 1)
    return entries.astype(jnp.int32)


def touch_ends(drawn, stream_key, least, largest):
    index_at = [jax.random.randint(jax.random.fold_in(stream_key, axis), (), 0, length) for axis, length in enumerate(drawn.shape)]
    longest = drawn.shape.index(max(drawn.shape))
    beside = index_at[:longest] + [(index_at[longest] + 1) % drawn.shape[longest]] + index_at[longest + 1:]
    return drawn.at[tuple(index_at)].set(least).at[tuple(beside)].set(largest)


def steps_of(own_key, shape, shards, least, largest):
    level = 1.0
    for position, blocks in shards:
        steps = jax.random.uniform(jax.random.fold_in(jax.random.fold_in(own_key, 6), position), (blocks,), jnp.float32, least / len(shards), largest / len(shards))
        level = level * jnp.repeat(jnp.exp(steps), shape[position] // blocks).reshape((-1,) + (1,) * (len(shape) - 1 - position))
    return level


def bell_draw(own_key, extent, deviation, reach, cuts=(), kind=jnp.bfloat16):
    values = deviation * jax.random.normal(own_key, extent, jnp.float32)
    if cuts:
        values = values * steps_of(own_key, extent, cuts, -0.22, 0.18)
    return jnp.clip(values, -reach, reach).astype(kind)


def setup_inputs(seed: int = 0) -> dict:
    splits = jax.random.split(jax.random.key(seed), 13)
    return {
        "dofs": bell_draw(splits[0], (QUANT, BASIS, ELEMS), 1.0, 6.0, ((2, 128),), jnp.float32),
        "star": bell_draw(splits[1], (3, QUANT, QUANT, ELEMS), 0.1, 0.6, ((3, 128),), jnp.float32),
        "flux_minus": bell_draw(splits[2], (4, QUANT, QUANT, ELEMS), 0.1, 0.6, ((3, 128),), jnp.float32),
        "flux_plus": bell_draw(splits[3], (4, QUANT, QUANT, ELEMS), 0.1, 0.6, ((3, 128),), jnp.float32),
        "cluster": draw_cluster(jax.random.fold_in(splits[12], 71), 0),
        "neighbour": draw_neighbour(jax.random.fold_in(splits[12], 71), 0),
        "face_code": touch_ends(jax.random.randint(splits[6], (4, ELEMS), 0, 12), jax.random.fold_in(splits[6], 1), 0, 11).astype(jnp.int32),
        "send_list": touch_ends(jax.random.randint(splits[7], (2 * RADIUS, SENDS), 0, E_DEV), jax.random.fold_in(splits[7], 1), 0, E_DEV - 1).astype(jnp.int32),
        "stiffness": bell_draw(splits[8], (3, BASIS, BASIS), BASIS ** -0.5, 1.0, (), jnp.float32),
        "face_proj": bell_draw(splits[9], (4, FACE_BASIS, BASIS), BASIS ** -0.5, 1.0, (), jnp.float32),
        "face_lift": bell_draw(splits[10], (4, BASIS, FACE_BASIS), FACE_BASIS ** -0.5, 1.5, (), jnp.float32),
        "face_turn": bell_draw(splits[11], (3, FACE_BASIS, FACE_BASIS), FACE_BASIS ** -0.5, 1.5, (), jnp.float32),
    }


HIGH = lax.Precision.HIGHEST


def derivatives(field, star, stiffness):
    terms = [field]
    current = field
    for level in range(ORDER - 1):
        spread = jnp.einsum('dbc,qce->dqbe', stiffness, current, precision=HIGH)
        current = -jnp.einsum('dpqe,dqbe->pbe', star, spread, precision=HIGH)
        terms.append(current)
    return terms


def integral(terms, start, finish):
    total = terms[0] * (finish - start)
    for level in range(1, len(terms)):
        factor = (finish ** (level + 1) - start ** (level + 1)) / math.factorial(level + 1)
        total = total + terms[level] * factor
    return total


def update(field, own, nearby, elements, tables):
    star, minus, plus, codes = elements
    stiffness, face_proj, face_lift, face_turn = tables
    spread = jnp.einsum('dcb,qce->dqbe', stiffness, own, precision=HIGH)
    volume = jnp.einsum('dpqe,dqbe->pbe', star, spread, precision=HIGH)
    local = jnp.einsum('igc,qce->iqge', face_proj, own, precision=HIGH)
    local = jnp.einsum('ipqe,iqge->ipge', minus, local, precision=HIGH)
    local = jnp.einsum('ibg,ipge->pbe', face_lift, local, precision=HIGH)
    every = jnp.einsum('jgc,iqce->ijqge', face_proj, nearby, precision=HIGH)
    pick_face = (codes[:, None, :] // 3 == jnp.arange(4, dtype=jnp.int32)[None, :, None]).astype(field.dtype)
    chosen = jnp.einsum('ije,ijqge->iqge', pick_face, every, precision=HIGH)
    turned = jnp.einsum('hgk,iqke->ihqge', face_turn, chosen, precision=HIGH)
    pick_turn = (codes[:, None, :] % 3 == jnp.arange(3, dtype=jnp.int32)[None, :, None]).astype(field.dtype)
    chosen = jnp.einsum('ihe,ihqge->iqge', pick_turn, turned, precision=HIGH)
    remote = jnp.einsum('ipqe,iqge->ipge', plus, chosen, precision=HIGH)
    remote = jnp.einsum('ibg,ipge->pbe', face_lift, remote, precision=HIGH)
    return field + volume - local - remote


def reference(dofs, star, flux_minus, flux_plus, cluster, neighbour, face_code, send_list, stiffness, face_proj, face_lift, face_turn):
    tables = (stiffness, face_proj, face_lift, face_turn)
    count = ELEMS // E_DEV
    column = jnp.arange(ELEMS, dtype=jnp.int32)
    home = (column // E_DEV)[None, :]
    ghost = jnp.maximum(neighbour - E_DEV, 0)
    which = ghost // SEND
    place = ghost % SEND
    offset = jnp.where(which < RADIUS, which - RADIUS, which - RADIUS + 1)
    source = jnp.clip(home - offset, 0, count - 1)
    flat_list = send_list.reshape(-1)
    remote_slot = flat_list[which * SENDS + source * SEND + place]
    partner = jnp.where(neighbour < E_DEV, home * E_DEV + neighbour, source * E_DEV + remote_slot).astype(jnp.int32)

    def block(array, index):
        return lax.dynamic_slice_in_dim(array, index * E_DEV, E_DEV, axis=array.ndim - 1)

    def whole(stacked):
        moved_axes = jnp.moveaxis(stacked, 0, -2)
        return moved_axes.reshape(moved_axes.shape[:-2] + (ELEMS,))

    def elements_of(index):
        return (block(star, index), block(flux_minus, index), block(flux_plus, index), block(face_code, index))

    def nearby(field, index):
        return jnp.moveaxis(jnp.take(field, block(partner, index), axis=2), 2, 0)

    indices = jnp.arange(count, dtype=jnp.int32)

    def first(index):
        terms = derivatives(block(dofs, index), block(star, index), stiffness)
        return jnp.stack([integral(terms, 0.0, 1.0), integral(terms, 1.0, 2.0)])

    integrals = whole(lax.map(first, indices))
    early = integrals[0]
    later = integrals[1]

    def second(index):
        elements = elements_of(index)
        fast = block(cluster, index) == 0
        start = block(dofs, index)
        stepped = update(start, block(early, index), nearby(early, index), elements, tables)
        moved = jnp.where(fast, stepped, start)
        fresh = integral(derivatives(moved, elements[0], stiffness), 0.0, 1.0)
        late = jnp.where(fast, fresh, block(later, index))
        return jnp.stack([moved, late])

    middle = whole(lax.map(second, indices))
    moved_all = middle[0]
    late_all = middle[1]

    def third(index):
        elements = elements_of(index)
        kinds = block(cluster, index)
        start = block(dofs, index)
        own_late = block(late_all, index)
        near_late = nearby(late_all, index)
        quick = update(block(moved_all, index), own_late, near_late, elements, tables)
        steady = update(start, block(early, index) + own_late, nearby(early, index) + near_late, elements, tables)
        return jnp.where(kinds == 0, quick, jnp.where(kinds == 1, steady, start))

    return whole(lax.map(third, indices))
```

```python
import math

import jax
import jax.numpy as jnp
from jax import lax
from jax.experimental import pallas as pl
from jax.experimental.pallas import tpu as pltpu
from jax.sharding import PartitionSpec as P

ORDER = 5
E = 384
F = 128
Q = 9
C = 40
G = 16
GHOST = 256
LANES = 128

HIGH = lax.Precision.HIGHEST
F32 = jnp.float32
BF16 = jnp.bfloat16


def iota(shape, dim):
    return lax.broadcasted_iota(jnp.int32, shape, dim)


def exact(a, b, dims=(((1,), (0,)), ((), ()))):
    return lax.dot_general(a, b, dims, precision=HIGH, preferred_element_type=F32)


def mxu(a, b, dims=(((1,), (0,)), ((), ()))):
    return lax.dot_general(a, b, dims, preferred_element_type=F32)


def split(x):
    high = x.astype(BF16)
    return high, (x - high.astype(F32)).astype(BF16)


def lane_gather(x, at):
    numbers = lax.GatherDimensionNumbers(
        offset_dims=(),
        collapsed_slice_dims=(1,),
        start_index_map=(1,),
        operand_batching_dims=(0,),
        start_indices_batching_dims=(0,),
    )
    mode = lax.GatherScatterMode.PROMISE_IN_BOUNDS
    return lax.gather(x, at[..., None], numbers, (1, 1), mode=mode)


def lanes_of(width):
    return [slice(at, at + LANES) for at in range(0, width, LANES)]


def stiffness_rows(stiffness, transposed, sign, pad_ref):
    total = jnp.zeros((35, 256), F32)
    for d in range(3):
        place = (iota((35, 256), 1) % 128 == d * C + iota((35, 256), 0)).astype(F32)
        dims = (((0,), (0,)), ((), ())) if transposed else (((1,), (0,)), ((), ()))
        total = total + exact(stiffness[d], place, dims)
    pad_ref[32:C, :] = jnp.zeros((8, 256), F32)
    pad_ref[0:35, :] = total * sign
    padded = pad_ref[...]
    high, low = split(padded)
    low = jnp.where(iota((C, 256), 1) < 128, low.astype(F32), 0.0)
    return jnp.concatenate([high.astype(F32), low], axis=0).astype(BF16)


def three(rows, first):
    high, low = split(rows)
    keep = iota(rows.shape, 1) < first
    return jnp.where(keep, high.astype(F32), low.astype(F32)).astype(BF16)


def three_parts(x):
    high, low = split(x)
    return jnp.concatenate([high, low, high], axis=0)


def padded48(x):
    return jnp.concatenate([x, jnp.zeros((8, x.shape[1]), F32)], axis=0)


def star_times(star_ref, source, p, width):
    columns = []
    for at in lanes_of(width):
        values = [source[q, :, at] for q in range(Q)]
        parts = []
        for d in range(3):
            total = star_ref[d, p, 0:1, at] * values[0]
            for q in range(1, Q):
                total = total + star_ref[d, p, q : q + 1, at] * values[q]
            parts.append(total)
        parts.append(jnp.zeros((8, LANES), F32))
        high, low = split(jnp.concatenate(parts, axis=0))
        columns.append(jnp.concatenate([high, low], axis=0))
    return jnp.concatenate(columns, axis=1) if len(columns) > 1 else columns[0]


def halves(out):
    return out[:C] + out[C:]


def taylor(star_ref, rows, cur_ref, width, add):
    for level in range(ORDER - 1):
        source, target = cur_ref.at[level % 2], cur_ref.at[(level + 1) % 2]

        @pl.loop(0, Q)
        def _(p):
            value = halves(mxu(rows, star_times(star_ref, source, p, width)))
            target[p] = value
            add(level, p, value)


def flux(coefficients, source, target, width, accumulate):
    @pl.loop(0, 4)
    def _(i):
        rows = pl.ds(pl.multiple_of(i * G, G), G)
        for at in lanes_of(width):
            values = [source[q, rows, at] for q in range(Q)]
            for p in range(Q):
                total = coefficients[i, p, 0:1, at] * values[0]
                for q in range(1, Q):
                    total = total + coefficients[i, p, q : q + 1, at] * values[q]
                if accumulate:
                    total = target[p, rows, at] + total
                target[p, rows, at] = total


def own_faces(own, proj_rows, face_ref, width):
    @pl.loop(0, Q)
    def _(q):
        face_ref[q] = mxu(proj_rows, three_parts(padded48(own[q])))


def near_faces(parts, neighbour, codes, turn_rows, near_ref, face_ref, width):
    for i in range(4):
        total = None
        wanted = neighbour[i : i + 1, :]
        for arrays, first, mask in parts:
            columns = arrays[0].shape[1]
            hit = iota((columns, width), 0) + first == wanted
            if mask is not None:
                hit = hit & mask
            pick = jnp.where(hit, 1.0, 0.0).astype(BF16)
            for array in arrays:
                piece = mxu(array, pick)
                total = piece if total is None else total + piece
        near_ref[...] = total
        code = codes[i : i + 1, :]

        @pl.loop(0, Q)
        def _(q):
            rows = pl.ds(pl.multiple_of(q * C, 8), C)
            every = mxu(turn_rows, three_parts(padded48(near_ref[rows, :])))
            chosen = every[0:G]
            for k in range(1, 12):
                chosen = jnp.where(code == k, every[k * G : (k + 1) * G], chosen)
            face_ref[q, i * G : (i + 1) * G, :] = chosen


def flat(x):
    return x.reshape(Q * C, x.shape[-1])


def first_kernel(core, dofs, star, stiffness, send_list, early, later, inner, outer, cur, pad):
    for q in range(Q):
        cur[0, q, 32:C, :] = jnp.zeros((8, E), F32)
        cur[0, q, 0:35, :] = dofs[q]
        early[q] = cur[0, q]
        later[q] = cur[0, q]
    rows = stiffness_rows(stiffness, False, -1.0, pad)

    def add(level, p, value):
        k = level + 1
        early[p] = early[p] + value * (1.0 / math.factorial(k + 1))
        later[p] = later[p] + value * ((2.0 ** (k + 1) - 1.0) / math.factorial(k + 1))

    taylor(star, rows, cur, E, add)
    pick = send_pick(core, send_list)
    high, low = split(flat(early[...]))
    sent = mxu(high, pick) + mxu(low, pick)
    inner[...] = sent[:, :LANES]
    outer[...] = sent[:, LANES:]


def send_pick(core, send_list):
    spread = (iota((32, GHOST), 0) == iota((32, GHOST), 1) % 32).astype(F32)
    table = exact(send_list[...].astype(F32), spread)
    message = iota((8, GHOST), 1) // 32
    row = jnp.where(message < 4, 3 - message, jnp.where(message == 4, 4, 12 - message))
    row = jnp.where(core[0] == 0, row, 7 - row)
    wanted = jnp.sum(jnp.where(row == iota((8, GHOST), 0), table, 0.0), axis=0, keepdims=True)
    wanted = wanted.astype(jnp.int32)
    return jnp.where(iota((E, GHOST), 0) == wanted, 1.0, 0.0).astype(BF16)


def ghost_columns(core, neighbour):
    ghost = neighbour - E
    o = ghost >> 5
    offset = jnp.where(o < 4, o - 4, o - 3)
    offset = jnp.where(core[0] == 0, offset, -offset)
    place = jnp.where(offset > 0, (5 - offset) & 3, 3 - offset)
    return jnp.where(neighbour < E, neighbour, E + place * 32 + (ghost & 31))


def fast_rows(cluster):
    fast = cluster == 0
    before = (iota((E, E), 0) < iota((E, E), 1)).astype(F32).astype(BF16)
    rank = mxu(jnp.where(fast, 1.0, 0.0).astype(BF16), before).astype(jnp.int32)
    return jnp.where((iota((F, E), 0) == rank) & fast, 1.0, 0.0).astype(BF16)


def second_kernel(
    core, dofs, star, minus, plus, cluster, neighbour, codes, early,
    stiffness, proj, lift, turn,
    field, star_f, plus_f, lines_f, scatter, nb_all, volume_rows, lift_rows, turn_rows, proj_rows,
    minus_f, early_f, face, flow, near, pad, pad_lift, pad_turn,
):
    volume_rows[...] = stiffness_rows(stiffness, True, 1.0, pad)
    pad_lift[32:C, :] = jnp.zeros((8, 192), F32)
    total = jnp.zeros((35, 192), F32)
    for i in range(4):
        place = (iota((15, 192), 1) % 64 == i * G + iota((15, 192), 0)).astype(F32)
        total = total - exact(lift[i], place)
    pad_lift[0:35, :] = total
    lift_rows[...] = three(pad_lift[...], 128)
    place = (iota((35, 144), 1) % 48 == iota((35, 144), 0)).astype(F32)
    pad_turn[...] = jnp.zeros((192, 144), F32)
    for i in range(4):
        pad_turn[i * G : i * G + 15, :] = exact(proj[i], place)
    proj_rows[...] = three(pad_turn[0:64, :], 96)
    projs = [exact(proj[i], place) for i in range(4)]
    for i in range(4):
        for h in range(3):
            at = (3 * i + h) * G
            pad_turn[at : at + 15, :] = exact(turn[h], projs[i])
    turn_rows[...] = three(pad_turn[...], 96)

    kinds = cluster[...]
    picks = fast_rows(kinds)
    scatter[...] = picks
    column = iota((8, E), 1)
    which = jnp.where(iota((8, E), 0) == 0, column // LANES, column % LANES).astype(F32).astype(BF16)
    found = mxu(which, picks, (((1,), (1,)), ((), ()))).astype(jnp.int32)
    block, lane = found[0:1], found[1:2]

    def take(x):
        r = x.shape[0]
        at = jnp.broadcast_to(lane, (r, F))
        got = [lane_gather(x[:, s], at) for s in lanes_of(E)]
        return jnp.where(block == 0, got[0], jnp.where(block == 1, got[1], got[2]))

    for q in range(Q):
        field[q, 32:C, :] = jnp.zeros((8, F), F32)
        field[q, 0:32, :] = take(dofs[q, 0:32, :])
        field[q, 32:35, :] = take(dofs[q, 32:35, :])
        early_f[q] = take(early[q])

    @pl.loop(0, Q)
    def _(p):
        for d in range(3):
            star_f[d, p, 0:8, :] = take(star[d, p, 0:8, :])
            star_f[d, p, 8:9, :] = take(star[d, p, 8:9, :])
        for i in range(4):
            minus_f[i, p, 0:8, :] = take(minus[i, p, 0:8, :])
            minus_f[i, p, 8:9, :] = take(minus[i, p, 8:9, :])
            plus_f[i, p, 0:8, :] = take(plus[i, p, 0:8, :])
            plus_f[i, p, 8:9, :] = take(plus[i, p, 8:9, :])

    table = ghost_columns(core, neighbour[...])
    nb_all[...] = table
    nb = take(table)
    code = take(codes[...])
    lines_f[0:4, :] = nb
    lines_f[4:8, :] = code

    own_faces(early_f, proj_rows[...], face, F)
    flux(minus_f, face, flow, F, False)
    near_faces([(split(flat(early[...])), 0, None)], nb, code, turn_rows[...], near, face, F)
    flux(plus_f, face, flow, F, True)

    @pl.loop(0, Q)
    def _(p):
        field[p] = (
            field[p]
            + halves(mxu(volume_rows[...], star_times(star_f, early_f, p, F)))
            + mxu(lift_rows[...], three_parts(flow[p]))
        )


def third_kernel(
    core, stiffness, send_list, a, b, q_in, field, star_f, plus_f, lines_f, scatter, cluster, later, dofs,
    lift_rows, turn_rows,
    moved, late, inner, outer,
    late_f, cur, face, flow, near, pad,
):
    ghosts = ghost_array(a, b, q_in)
    near_faces([(split(ghosts), E, None)], lines_f[0:4, :], lines_f[4:8, :], turn_rows[...], near, face, F)
    flux(plus_f, face, flow, F, False)
    for p in range(Q):
        value = field[p] + mxu(lift_rows[...], three_parts(flow[p]))
        cur[0, p] = value
        late_f[0, p] = value
        late_f[1, p] = value
    rows = stiffness_rows(stiffness, False, -1.0, pad)

    def add(level, p, value):
        late_f[0, p] = late_f[0, p] + value * (1.0 / math.factorial(level + 2))

    taylor(star_f, rows, cur, F, add)
    fast = cluster[...] == 0
    picks = scatter[...]
    for p in range(Q):
        high, low = split(late_f[0, p])
        late[p] = jnp.where(fast, mxu(high, picks) + mxu(low, picks), later[p])
    pick = send_pick(core, send_list)
    high, low = split(flat(late[...]))
    sent = mxu(high, pick) + mxu(low, pick)
    inner[...] = sent[:, :LANES]
    outer[...] = sent[:, LANES:]
    for p in range(Q):
        moved[p] = late_f[1, p]


def ghost_array(a, b, q_in):
    part = iota((Q * C, LANES), 1) // 32
    mine = jnp.where((part == 0) | (part == 3), a[...], b[...])
    return jnp.concatenate([mine, q_in[...]], axis=1)


def fourth_kernel(
    dofs, star, minus, plus, cluster, nb_all, codes, early, later, late, moved, scatter,
    a, b, q_in, volume_rows, lift_rows, turn_rows, proj_rows,
    out, own, face, flow, near,
):
    kinds = cluster[...]
    fast = kinds == 0
    picks = scatter[...]
    for p in range(Q):
        own[p] = jnp.where(fast, late[p], early[p] + later[p])
        high, low = split(moved[p])
        out[p] = jnp.where(fast, mxu(high, picks) + mxu(low, picks), 0.0)
        out[p, 0:35, :] = jnp.where(fast, out[p, 0:35, :], dofs[p])
    own_faces(own, proj_rows[...], face, E)
    flux(minus, face, flow, E, False)
    ghosts = ghost_array(a, b, q_in)
    near_faces(
        [
            (split(flat(late[...])), 0, None),
            (split(flat(early[...])), 0, kinds == 1),
            (split(ghosts), E, kinds == 1),
        ],
        nb_all[...], codes[...], turn_rows[...], near, face, E,
    )
    flux(plus, face, flow, E, True)

    @pl.loop(0, Q)
    def _(p):
        out[p] = (
            out[p]
            + halves(mxu(volume_rows[...], star_times(star, own, p, E)))
            + mxu(lift_rows[...], three_parts(flow[p]))
        )


def fifth_kernel(
    dofs, plus, cluster, nb_all, codes, partial, a, b, q_in, lift_rows, turn_rows,
    out, face, flow, near,
):
    ghosts = ghost_array(a, b, q_in)
    near_faces([(split(ghosts), E, None)], nb_all[...], codes[...], turn_rows[...], near, face, E)
    flux(plus, face, flow, E, False)
    active = cluster[...] < 2
    for p in range(Q):
        value = partial[p] + mxu(lift_rows[...], three_parts(flow[p]))
        out[p] = jnp.where(active, value[0:35], dofs[p])


def call(kernel, outs, args, scratch, scalars=0):
    vmem = pl.BlockSpec(memory_space=pltpu.VMEM)
    smem = pl.BlockSpec(memory_space=pltpu.SMEM)
    return pl.pallas_call(
        kernel,
        out_shape=[jax.ShapeDtypeStruct(*o) for o in outs],
        in_specs=[smem] * scalars + [vmem] * (len(args) - scalars),
        out_specs=[vmem] * len(outs),
        scratch_shapes=[pltpu.VMEM(*s) for s in scratch],
        compiler_params=pltpu.CompilerParams(vmem_limit_bytes=48 * 1024 * 1024),
        name=kernel.__name__,
    )(*args)


def exchange(inner, outer):
    count = lax.axis_size("dom")
    chips = count // 2

    def along(reach):
        def target(device):
            chip, core = device // 2, device % 2
            return 2 * ((chip + (reach if core == 0 else -reach)) % chips) + core

        return [(device, target(device)) for device in range(count)]

    pair = [(device, device ^ 1) for device in range(count)]
    part = iota((1, LANES), 1) // 32
    beside = lax.ppermute(inner, "dom", pair)
    a = lax.ppermute(jnp.where(part < 2, beside, outer), "dom", along(1))
    b = lax.ppermute(jnp.where(part < 2, outer, beside), "dom", along(2))
    back = jnp.where(part == 0, outer, jnp.where(part == 3, b, a))
    return a, b, lax.ppermute(back, "dom", pair)


def body(
    dofs,
    star,
    flux_minus,
    flux_plus,
    cluster,
    neighbour,
    face_code,
    send_list,
    stiffness,
    face_proj,
    face_lift,
    face_turn,
):
    core = (lax.axis_index("dom") % 2).astype(jnp.int32).reshape(1)
    cluster = cluster.reshape(1, E)
    whole, compact, block = (Q, C, E), (Q, C, F), (Q * C, LANES)
    early, later, inner, outer = call(
        first_kernel,
        [(whole, F32), (whole, F32), (block, F32), (block, F32)],
        [core, dofs, star, stiffness, send_list],
        [((2,) + whole, F32), ((C, 256), F32)],
        1,
    )
    a, b, q_in = exchange(inner, outer)
    (
        field, star_f, plus_f, lines_f, scatter, nb_all, volume_rows, lift_rows, turn_rows, proj_rows
    ) = call(
        second_kernel,
        [
            (compact, F32), ((3, Q, Q, F), F32), ((4, Q, Q, F), F32), ((8, F), jnp.int32),
            ((F, E), BF16), ((4, E), jnp.int32),
            ((2 * C, 256), BF16), ((C, 192), BF16), ((192, 144), BF16), ((64, 144), BF16),
        ],
        [
            core, dofs, star, flux_minus, flux_plus, cluster, neighbour, face_code, early,
            stiffness, face_proj, face_lift, face_turn,
        ],
        [
            ((4, Q, Q, F), F32), (compact, F32), ((Q, 64, F), F32), ((Q, 64, F), F32),
            ((Q * C, F), F32), ((C, 256), F32), ((C, 192), F32), ((192, 144), F32),
        ],
        1,
    )
    moved, late, inner, outer = call(
        third_kernel,
        [(compact, F32), (whole, F32), (block, F32), (block, F32)],
        [
            core, stiffness, send_list, a, b, q_in, field, star_f, plus_f, lines_f, scatter, cluster,
            later, dofs, lift_rows, turn_rows,
        ],
        [
            ((2,) + compact, F32), ((2,) + compact, F32), ((Q, 64, F), F32), ((Q, 64, F), F32),
            ((Q * C, F), F32), ((C, 256), F32),
        ],
        1,
    )
    a2, b2, q2 = exchange(inner, outer)
    (partial,) = call(
        fourth_kernel,
        [(whole, F32)],
        [
            dofs, star, flux_minus, flux_plus, cluster, nb_all, face_code, early, later, late, moved,
            scatter, a, b, q_in, volume_rows, lift_rows, turn_rows, proj_rows,
        ],
        [(whole, F32), ((Q, 64, E), F32), ((Q, 64, E), F32), ((Q * C, E), F32)],
    )
    (out,) = call(
        fifth_kernel,
        [((Q, 35, E), F32)],
        [dofs, flux_plus, cluster, nb_all, face_code, partial, a2, b2, q2, lift_rows, turn_rows],
        [((Q, 64, E), F32), ((Q, 64, E), F32), ((Q * C, E), F32)],
    )
    return out


def solution(mesh):
    return jax.shard_map(
        body,
        mesh=mesh,
        in_specs=(
            P(None, None, "dom"),
            P(None, None, None, "dom"),
            P(None, None, None, "dom"),
            P(None, None, None, "dom"),
            P("dom"),
            P(None, "dom"),
            P(None, "dom"),
            P(None, "dom"),
            P(),
            P(),
            P(),
            P(),
        ),
        out_specs=P(None, None, "dom"),
        check_vma=False,
    )
```

```python
import math

import jax
import jax.numpy as jnp
from jax import lax
from jax.experimental import pallas as pl
from jax.experimental.pallas import tpu as pltpu
from jax.sharding import PartitionSpec as P

ORDER = 5
E = 384
F = 128
Q = 9
C = 40
G = 16
GHOST = 256
LANES = 128

HIGH = lax.Precision.HIGHEST
F32 = jnp.float32
BF16 = jnp.bfloat16


def iota(shape, dim):
    return lax.broadcasted_iota(jnp.int32, shape, dim)


def exact(a, b, dims=(((1,), (0,)), ((), ()))):
    return lax.dot_general(a, b, dims, precision=HIGH, preferred_element_type=F32)


def mxu(a, b, dims=(((1,), (0,)), ((), ()))):
    return lax.dot_general(a, b, dims, preferred_element_type=F32)


def split(x):
    high = x.astype(BF16)
    return high, (x - high.astype(F32)).astype(BF16)


def lane_gather(x, at):
    numbers = lax.GatherDimensionNumbers(
        offset_dims=(),
        collapsed_slice_dims=(1,),
        start_index_map=(1,),
        operand_batching_dims=(0,),
        start_indices_batching_dims=(0,),
    )
    mode = lax.GatherScatterMode.PROMISE_IN_BOUNDS
    return lax.gather(x, at[..., None], numbers, (1, 1), mode=mode)


def lanes_of(width):
    return [slice(at, at + LANES) for at in range(0, width, LANES)]


def stiffness_rows(stiffness, transposed, sign, pad_ref):
    total = jnp.zeros((35, 256), F32)
    for d in range(3):
        place = (iota((35, 256), 1) % 128 == d * C + iota((35, 256), 0)).astype(F32)
        dims = (((0,), (0,)), ((), ())) if transposed else (((1,), (0,)), ((), ()))
        total = total + exact(stiffness[d], place, dims)
    pad_ref[32:C, :] = jnp.zeros((8, 256), F32)
    pad_ref[0:35, :] = total * sign
    padded = pad_ref[...]
    high, low = split(padded)
    low = jnp.where(iota((C, 256), 1) < 128, low.astype(F32), 0.0)
    return jnp.concatenate([high.astype(F32), low], axis=0).astype(BF16)


def three(rows, first):
    high, low = split(rows)
    keep = iota(rows.shape, 1) < first
    return jnp.where(keep, high.astype(F32), low.astype(F32)).astype(BF16)


def three_parts(x):
    high, low = split(x)
    return jnp.concatenate([high, low, high], axis=0)


def padded48(x):
    return jnp.concatenate([x, jnp.zeros((8, x.shape[1]), F32)], axis=0)


def star_times(star_ref, source, p, width):
    columns = []
    for at in lanes_of(width):
        values = [source[q, :, at] for q in range(Q)]
        parts = []
        for d in range(3):
            total = star_ref[p, 0, d : d + 1, at] * values[0]
            for q in range(1, Q):
                total = total + star_ref[p, q, d : d + 1, at] * values[q]
            parts.append(total)
        parts.append(jnp.zeros((8, LANES), F32))
        high, low = split(jnp.concatenate(parts, axis=0))
        columns.append(jnp.concatenate([high, low], axis=0))
    return jnp.concatenate(columns, axis=1) if len(columns) > 1 else columns[0]


def halves(out):
    return out[:C] + out[C:]


def taylor(star_ref, rows, cur_ref, width, add):
    for level in range(ORDER - 1):
        source, target = cur_ref.at[level % 2], cur_ref.at[(level + 1) % 2]
        for p in range(Q):
            value = halves(mxu(rows, star_times(star_ref, source, p, width)))
            target[p] = value
            add(level, p, value)


def flux(coefficients, source, target, width, accumulate):
    for i in range(4):
        rows = slice(i * G, (i + 1) * G)
        for at in lanes_of(width):
            values = [source[q, rows, at] for q in range(Q)]
            for p in range(Q):
                total = coefficients[p, 0, i : i + 1, at] * values[0]
                for q in range(1, Q):
                    total = total + coefficients[p, q, i : i + 1, at] * values[q]
                if accumulate:
                    total = target[p, rows, at] + total
                target[p, rows, at] = total


def own_faces(own, proj_rows, face_ref, width):
    for q in range(Q):
        face_ref[q] = mxu(proj_rows, three_parts(padded48(own[q])))


def beside(rows):
    return jnp.concatenate([rows[i : i + 1, :] for i in range(4)], axis=1)


def near_faces(parts, neighbour, codes, turn_rows, near_ref, face_ref, width):
    total = None
    wanted = beside(neighbour)
    for arrays, first, mask in parts:
        columns = arrays[0].shape[1]
        hit = iota((columns, 4 * width), 0) + first == wanted
        if mask is not None:
            hit = hit & jnp.concatenate([mask] * 4, axis=1)
        pick = jnp.where(hit, 1.0, 0.0).astype(BF16)
        for array in arrays:
            piece = mxu(array, pick)
            total = piece if total is None else total + piece
    near_ref[...] = total
    code = beside(codes)
    for q in range(Q):
        every = mxu(turn_rows, three_parts(padded48(near_ref[q * C : (q + 1) * C, :])))
        chosen = every[0:G]
        for k in range(1, 12):
            chosen = jnp.where(code == k, every[k * G : (k + 1) * G], chosen)
        for i in range(4):
            face_ref[q, i * G : (i + 1) * G, :] = chosen[:, i * width : (i + 1) * width]


def flat(x):
    return x.reshape(Q * C, x.shape[-1])


def first_kernel(
    core, dofs_in, star_in, stiffness_in, send_list_in,
    early, later, inner, outer,
    cur, pad, dofs, star, stiffness, send_list, done,
):
    small = [
        pltpu.make_async_copy(stiffness_in, stiffness, done.at[18]),
        pltpu.make_async_copy(send_list_in, send_list, done.at[19]),
    ]
    fields = [pltpu.make_async_copy(dofs_in.at[q], dofs.at[q], done.at[q]) for q in range(Q)]
    stars = [pltpu.make_async_copy(star_in.at[p], star.at[p], done.at[Q + p]) for p in range(Q)]
    for copy in small + fields + stars:
        copy.start()
    for q in range(Q):
        cur[0, q, 32:C, :] = jnp.zeros((8, E), F32)
    small[0].wait()
    small[1].wait()
    rows = stiffness_rows(stiffness, False, -1.0, pad)
    for q in range(Q):
        fields[q].wait()
        cur[0, q, 0:35, :] = dofs[q]
        early[q] = cur[0, q]
        later[q] = cur[0, q]

    def add(level, p, value):
        k = level + 1
        early[p] = early[p] + value * (1.0 / math.factorial(k + 1))
        later[p] = later[p] + value * ((2.0 ** (k + 1) - 1.0) / math.factorial(k + 1))

    for copy in stars:
        copy.wait()
    taylor(star, rows, cur, E, add)
    pick = send_pick(core, send_list)
    high, low = split(flat(early[...]))
    sent = mxu(high, pick) + mxu(low, pick)
    inner[...] = sent[:, :LANES]
    outer[...] = sent[:, LANES:]


def send_pick(core, send_list):
    spread = (iota((32, GHOST), 0) == iota((32, GHOST), 1) % 32).astype(F32)
    table = exact(send_list[...].astype(F32), spread)
    message = iota((8, GHOST), 1) // 32
    row = jnp.where(message < 4, 3 - message, jnp.where(message == 4, 4, 12 - message))
    row = jnp.where(core[0] == 0, row, 7 - row)
    wanted = jnp.sum(jnp.where(row == iota((8, GHOST), 0), table, 0.0), axis=0, keepdims=True)
    wanted = wanted.astype(jnp.int32)
    return jnp.where(iota((E, GHOST), 0) == wanted, 1.0, 0.0).astype(BF16)


def ghost_columns(core, neighbour):
    ghost = neighbour - E
    o = ghost >> 5
    offset = jnp.where(o < 4, o - 4, o - 3)
    offset = jnp.where(core[0] == 0, offset, -offset)
    place = jnp.where(offset > 0, (5 - offset) & 3, 3 - offset)
    return jnp.where(neighbour < E, neighbour, E + place * 32 + (ghost & 31))


def fast_rows(cluster):
    fast = cluster == 0
    before = (iota((E, E), 0) < iota((E, E), 1)).astype(F32).astype(BF16)
    rank = mxu(jnp.where(fast, 1.0, 0.0).astype(BF16), before).astype(jnp.int32)
    return jnp.where((iota((F, E), 0) == rank) & fast, 1.0, 0.0).astype(BF16)


def second_kernel(
    core, dofs, star, minus, plus, cluster, neighbour, codes, early,
    stiffness, proj, lift, turn, outer,
    field, star_f, plus_f, lines_f, scatter, nb_all, volume_rows, lift_rows, turn_rows, proj_rows, kept,
    minus_f, early_f, face, flow, near, pad, pad_lift, pad_turn,
):
    kept[...] = outer[...]
    volume_rows[...] = stiffness_rows(stiffness, True, 1.0, pad)
    pad_lift[32:C, :] = jnp.zeros((8, 192), F32)
    total = jnp.zeros((35, 192), F32)
    for i in range(4):
        place = (iota((15, 192), 1) % 64 == i * G + iota((15, 192), 0)).astype(F32)
        total = total - exact(lift[i], place)
    pad_lift[0:35, :] = total
    lift_rows[...] = three(pad_lift[...], 128)
    place = (iota((35, 144), 1) % 48 == iota((35, 144), 0)).astype(F32)
    pad_turn[...] = jnp.zeros((192, 144), F32)
    for i in range(4):
        pad_turn[i * G : i * G + 15, :] = exact(proj[i], place)
    proj_rows[...] = three(pad_turn[0:64, :], 96)
    projs = [exact(proj[i], place) for i in range(4)]
    for i in range(4):
        for h in range(3):
            at = (3 * i + h) * G
            pad_turn[at : at + 15, :] = exact(turn[h], projs[i])
    turn_rows[...] = three(pad_turn[...], 96)

    kinds = cluster[...]
    picks = fast_rows(kinds)
    scatter[...] = picks
    column = iota((8, E), 1)
    which = jnp.where(iota((8, E), 0) == 0, column // LANES, column % LANES).astype(F32).astype(BF16)
    found = mxu(which, picks, (((1,), (1,)), ((), ()))).astype(jnp.int32)
    block, lane = found[0:1], found[1:2]

    def take(x):
        r = x.shape[0]
        at = jnp.broadcast_to(lane, (r, F))
        got = [lane_gather(x[:, s], at) for s in lanes_of(E)]
        return jnp.where(block == 0, got[0], jnp.where(block == 1, got[1], got[2]))

    for q in range(Q):
        field[q, 32:C, :] = jnp.zeros((8, F), F32)
        field[q, 0:32, :] = take(dofs[q, 0:32, :])
        field[q, 32:35, :] = take(dofs[q, 32:35, :])
        early_f[q] = take(early[q])

    @pl.loop(0, Q)
    def _(p):
        for q in range(Q):
            star_f[p, q] = take(star[p, q])
            minus_f[p, q] = take(minus[p, q])
            plus_f[p, q] = take(plus[p, q])

    table = ghost_columns(core, neighbour[...])
    nb_all[...] = table
    nb = take(table)
    code = take(codes[...])
    lines_f[0:4, :] = nb
    lines_f[4:8, :] = code

    own_faces(early_f, proj_rows[...], face, F)
    flux(minus_f, face, flow, F, False)
    near_faces([(split(flat(early[...])), 0, None)], nb, code, turn_rows[...], near, face, F)
    flux(plus_f, face, flow, F, True)

    for p in range(Q):
        field[p] = (
            field[p]
            + halves(mxu(volume_rows[...], star_times(star_f, early_f, p, F)))
            + mxu(lift_rows[...], three_parts(flow[p]))
        )


def third_kernel(
    core, stiffness, send_list, a, b, q_in, field, star_f, plus_f, lines_f, scatter, cluster, later, dofs,
    lift_rows, turn_rows,
    moved, late, inner, outer,
    late_f, cur, face, flow, near, pad,
):
    ghosts = ghost_array(a, b, q_in)
    near_faces([(split(ghosts), E, None)], lines_f[0:4, :], lines_f[4:8, :], turn_rows[...], near, face, F)
    flux(plus_f, face, flow, F, False)
    for p in range(Q):
        value = field[p] + mxu(lift_rows[...], three_parts(flow[p]))
        cur[0, p] = value
        late_f[0, p] = value
        late_f[1, p] = value
    rows = stiffness_rows(stiffness, False, -1.0, pad)

    def add(level, p, value):
        late_f[0, p] = late_f[0, p] + value * (1.0 / math.factorial(level + 2))

    taylor(star_f, rows, cur, F, add)
    fast = cluster[...] == 0
    picks = scatter[...]
    for p in range(Q):
        high, low = split(late_f[0, p])
        late[p] = jnp.where(fast, mxu(high, picks) + mxu(low, picks), later[p])
    pick = send_pick(core, send_list)
    high, low = split(flat(late[...]))
    sent = mxu(high, pick) + mxu(low, pick)
    inner[...] = sent[:, :LANES]
    outer[...] = sent[:, LANES:]
    for p in range(Q):
        moved[p] = late_f[1, p]


def ghost_array(a, b, q_in):
    part = iota((Q * C, LANES), 1) // 32
    mine = jnp.where((part == 0) | (part == 3), a[...], b[...])
    return jnp.concatenate([mine, q_in[...]], axis=1)


def fourth_kernel(
    dofs, star, minus, plus, cluster, nb_all, codes, early, later, late, moved, scatter,
    a, b, q_in, volume_rows, lift_rows, turn_rows, proj_rows, outer,
    out, kept, own, face, flow, near,
):
    kept[...] = outer[...]
    kinds = cluster[...]
    fast = kinds == 0
    picks = scatter[...]
    for p in range(Q):
        own[p] = jnp.where(fast, late[p], early[p] + later[p])
        high, low = split(moved[p])
        out[p] = jnp.where(fast, mxu(high, picks) + mxu(low, picks), 0.0)
        out[p, 0:35, :] = jnp.where(fast, out[p, 0:35, :], dofs[p])
    own_faces(own, proj_rows[...], face, E)
    flux(minus, face, flow, E, False)
    ghosts = ghost_array(a, b, q_in)
    near_faces(
        [
            (split(flat(late[...])), 0, None),
            (split(flat(early[...])), 0, kinds == 1),
            (split(ghosts), E, kinds == 1),
        ],
        nb_all[...], codes[...], turn_rows[...], near, face, E,
    )
    flux(plus, face, flow, E, True)

    for p in range(Q):
        out[p] = (
            out[p]
            + halves(mxu(volume_rows[...], star_times(star, own, p, E)))
            + mxu(lift_rows[...], three_parts(flow[p]))
        )


def fifth_kernel(
    dofs, plus, cluster, nb_all, codes, partial, a, b, q_in, lift_rows, turn_rows,
    out, face, flow, near,
):
    ghosts = ghost_array(a, b, q_in)
    near_faces([(split(ghosts), E, None)], nb_all[...], codes[...], turn_rows[...], near, face, E)
    flux(plus, face, flow, E, False)
    active = cluster[...] < 2
    for p in range(Q):
        value = partial[p] + mxu(lift_rows[...], three_parts(flow[p]))
        out[p] = jnp.where(active, value[0:35], dofs[p])


def call(kernel, outs, args, scratch, scalars=0, copies=0, micros=5):
    vmem = pl.BlockSpec(memory_space=pltpu.VMEM)
    smem = pl.BlockSpec(memory_space=pltpu.SMEM)
    place = pl.BlockSpec(memory_space=pl.ANY) if copies else vmem
    if copies:
        args = args[:scalars] + [
            pltpu.with_memory_space_constraint(x, pltpu.HBM) for x in args[scalars:]
        ]
    return pl.pallas_call(
        kernel,
        out_shape=[jax.ShapeDtypeStruct(*o) for o in outs],
        in_specs=[smem] * scalars + [place] * (len(args) - scalars),
        out_specs=[vmem] * len(outs),
        scratch_shapes=[pltpu.VMEM(*s) for s in scratch]
        + ([pltpu.SemaphoreType.DMA((copies,))] if copies else []),
        compiler_params=pltpu.CompilerParams(vmem_limit_bytes=48 * 1024 * 1024),
        cost_estimate=pl.CostEstimate(
            flops=int(micros * 1e9), bytes_accessed=1 << 20, transcendentals=0
        ),
        name=kernel.__name__,
    )(*args)


def to_chips(inner, outer):
    count = lax.axis_size("dom")
    chips = count // 2

    def along(reach):
        def target(device):
            chip, core = device // 2, device % 2
            to = chip + (reach if core == 0 else -reach)
            return 2 * to + core if 0 <= to < chips else device ^ 1

        return [(device, target(device)) for device in range(count)]

    beside = to_pair(inner)
    first = iota((1, LANES), 1) < 64
    a = lax.ppermute(jnp.where(first, beside, outer), "dom", along(1))
    b = lax.ppermute(jnp.where(first, outer, beside), "dom", along(2))
    return a, b


def to_pair(value):
    count = lax.axis_size("dom")
    return lax.ppermute(value, "dom", [(device, device ^ 1) for device in range(count)])


def handed_on(outer, a, b):
    part = iota((1, LANES), 1) // 32
    return jnp.where(part == 0, outer, jnp.where(part == 3, b, a))


def body(
    dofs,
    star,
    flux_minus,
    flux_plus,
    cluster,
    neighbour,
    face_code,
    send_list,
    stiffness,
    face_proj,
    face_lift,
    face_turn,
):
    core = (lax.axis_index("dom") % 2).astype(jnp.int32).reshape(1)
    cluster = cluster.reshape(1, E)
    star, flux_minus, flux_plus = (
        jnp.transpose(x, (1, 2, 0, 3)) for x in (star, flux_minus, flux_plus)
    )
    whole, compact, block = (Q, C, E), (Q, C, F), (Q * C, LANES)
    early, later, inner, outer = call(
        first_kernel,
        [(whole, F32), (whole, F32), (block, F32), (block, F32)],
        [core, dofs, star, stiffness, send_list],
        [
            ((2,) + whole, F32), ((C, 256), F32), ((Q, 35, E), F32), ((Q, Q, 3, E), F32),
            ((3, 35, 35), F32), ((8, 32), jnp.int32),
        ],
        1,
        20,
    )
    a, b = to_chips(inner, outer)
    (
        field, star_f, plus_f, lines_f, scatter, nb_all, volume_rows, lift_rows, turn_rows, proj_rows,
        kept,
    ) = call(
        second_kernel,
        [
            (compact, F32), ((Q, Q, 3, F), F32), ((Q, Q, 4, F), F32), ((8, F), jnp.int32),
            ((F, E), BF16), ((4, E), jnp.int32),
            ((2 * C, 256), BF16), ((C, 192), BF16), ((192, 144), BF16), ((64, 144), BF16),
            (block, F32),
        ],
        [
            core, dofs, star, flux_minus, flux_plus, cluster, neighbour, face_code, early,
            stiffness, face_proj, face_lift, face_turn, outer,
        ],
        [
            ((Q, Q, 4, F), F32), (compact, F32), ((Q, 64, F), F32), ((Q, 64, F), F32),
            ((Q * C, 4 * F), F32), ((C, 256), F32), ((C, 192), F32), ((192, 144), F32),
        ],
        1,
    )
    q_in = to_pair(handed_on(kept, a, b))
    moved, late, inner, outer = call(
        third_kernel,
        [(compact, F32), (whole, F32), (block, F32), (block, F32)],
        [
            core, stiffness, send_list, a, b, q_in, field, star_f, plus_f, lines_f, scatter, cluster,
            later, dofs, lift_rows, turn_rows,
        ],
        [
            ((2,) + compact, F32), ((2,) + compact, F32), ((Q, 64, F), F32), ((Q, 64, F), F32),
            ((Q * C, 4 * F), F32), ((C, 256), F32),
        ],
        1,
    )
    a2, b2 = to_chips(inner, outer)
    partial, kept = call(
        fourth_kernel,
        [(whole, F32), (block, F32)],
        [
            dofs, star, flux_minus, flux_plus, cluster, nb_all, face_code, early, later, late, moved,
            scatter, a, b, q_in, volume_rows, lift_rows, turn_rows, proj_rows, outer,
        ],
        [(whole, F32), ((Q, 64, E), F32), ((Q, 64, E), F32), ((Q * C, 4 * E), F32)],
    )
    q2 = to_pair(handed_on(kept, a2, b2))
    (out,) = call(
        fifth_kernel,
        [((Q, 35, E), F32)],
        [dofs, flux_plus, cluster, nb_all, face_code, partial, a2, b2, q2, lift_rows, turn_rows],
        [((Q, 64, E), F32), ((Q, 64, E), F32), ((Q * C, 4 * E), F32)],
    )
    return out


def solution(mesh):
    return jax.shard_map(
        body,
        mesh=mesh,
        in_specs=(
            P(None, None, "dom"),
            P(None, None, None, "dom"),
            P(None, None, None, "dom"),
            P(None, None, None, "dom"),
            P("dom"),
            P(None, "dom"),
            P(None, "dom"),
            P(None, "dom"),
            P(),
            P(),
            P(),
            P(),
        ),
        out_specs=P(None, None, "dom"),
        check_vma=False,
    )
```

```python
import math

import jax
import jax.numpy as jnp
from jax import lax
from jax.experimental import pallas as pl
from jax.experimental.pallas import tpu as pltpu
from jax.sharding import PartitionSpec as P

ORDER = 5
E = 384
F = 128
Q = 9
C = 40
G = 16
GHOST = 256
LANES = 128

HIGH = lax.Precision.HIGHEST
F32 = jnp.float32
BF16 = jnp.bfloat16


def iota(shape, dim):
    return lax.broadcasted_iota(jnp.int32, shape, dim)


def exact(a, b, dims=(((1,), (0,)), ((), ()))):
    return lax.dot_general(a, b, dims, precision=HIGH, preferred_element_type=F32)


def mxu(a, b, dims=(((1,), (0,)), ((), ()))):
    return lax.dot_general(a, b, dims, preferred_element_type=F32)


def split(x):
    high = x.astype(BF16)
    return high, (x - high.astype(F32)).astype(BF16)


def lane_gather(x, at):
    numbers = lax.GatherDimensionNumbers(
        offset_dims=(),
        collapsed_slice_dims=(1,),
        start_index_map=(1,),
        operand_batching_dims=(0,),
        start_indices_batching_dims=(0,),
    )
    mode = lax.GatherScatterMode.PROMISE_IN_BOUNDS
    return lax.gather(x, at[..., None], numbers, (1, 1), mode=mode)


def both(x, right):
    high, low = split(x)
    return mxu(high, right) + mxu(low, right)


def lanes_of(width):
    return [slice(at, at + LANES) for at in range(0, width, LANES)]


def stiffness_rows(stiffness, transposed, sign, pad_ref):
    total = jnp.zeros((35, 256), F32)
    for d in range(3):
        place = (iota((35, 256), 1) % 128 == d * C + iota((35, 256), 0)).astype(F32)
        dims = (((0,), (0,)), ((), ())) if transposed else (((1,), (0,)), ((), ()))
        total = total + exact(stiffness[d], place, dims)
    pad_ref[32:C, :] = jnp.zeros((8, 256), F32)
    pad_ref[0:35, :] = total * sign
    padded = pad_ref[...]
    high, low = split(padded)
    low = jnp.where(iota((C, 256), 1) < 128, low.astype(F32), 0.0)
    return jnp.concatenate([high.astype(F32), low], axis=0).astype(BF16)


def three(rows, first):
    high, low = split(rows)
    keep = iota(rows.shape, 1) < first
    return jnp.where(keep, high.astype(F32), low.astype(F32)).astype(BF16)


def three_parts(x):
    high, low = split(x)
    return jnp.concatenate([high, low, high], axis=0)


def padded48(x):
    return jnp.concatenate([x, jnp.zeros((8, x.shape[1]), F32)], axis=0)


def star_times(star_ref, source, p, width):
    columns = []
    for at in lanes_of(width):
        values = [source[q, :, at] for q in range(Q)]
        parts = []
        for d in range(3):
            total = star_ref[p, 0, d : d + 1, at] * values[0]
            for q in range(1, Q):
                total = total + star_ref[p, q, d : d + 1, at] * values[q]
            parts.append(total)
        parts.append(jnp.zeros((8, LANES), F32))
        high, low = split(jnp.concatenate(parts, axis=0))
        columns.append(jnp.concatenate([high, low], axis=0))
    return jnp.concatenate(columns, axis=1) if len(columns) > 1 else columns[0]


def halves(out):
    return out[:C] + out[C:]


def taylor(star_ref, rows, cur_ref, width, add):
    for level in range(ORDER - 1):
        source, target = cur_ref.at[level % 2], cur_ref.at[(level + 1) % 2]
        for p in range(Q):
            value = halves(mxu(rows, star_times(star_ref, source, p, width)))
            target[p] = value
            add(level, p, value)


def flux(coefficients, source, target, width, accumulate):
    for i in range(4):
        rows = slice(i * G, (i + 1) * G)
        for at in lanes_of(width):
            values = [source[q, rows, at] for q in range(Q)]
            for p in range(Q):
                total = coefficients[p, 0, i : i + 1, at] * values[0]
                for q in range(1, Q):
                    total = total + coefficients[p, q, i : i + 1, at] * values[q]
                if accumulate:
                    total = target[p, rows, at] + total
                target[p, rows, at] = total


def own_faces(own, proj_rows, face_ref, width):
    for q in range(Q):
        face_ref[q] = mxu(proj_rows, three_parts(padded48(own[q])))


def beside(rows):
    return jnp.concatenate([rows[i : i + 1, :] for i in range(4)], axis=1)


def gathered(parts, neighbour, width, total=None):
    wanted = beside(neighbour)
    for arrays, first, mask in parts:
        columns = arrays[0].shape[1]
        hit = iota((columns, 4 * width), 0) + first == wanted
        if mask is not None:
            hit = hit & jnp.concatenate([mask] * 4, axis=1)
        pick = jnp.where(hit, 1.0, 0.0).astype(BF16)
        for array in arrays:
            piece = mxu(array, pick)
            total = piece if total is None else total + piece
    return total


def near_faces(near_ref, codes, turn_rows, face_ref, width):
    code = beside(codes)
    for q in range(Q):
        every = mxu(turn_rows, three_parts(padded48(near_ref[q * C : (q + 1) * C, :])))
        chosen = every[0:G]
        for k in range(1, 12):
            chosen = jnp.where(code == k, every[k * G : (k + 1) * G], chosen)
        for i in range(4):
            face_ref[q, i * G : (i + 1) * G, :] = chosen[:, i * width : (i + 1) * width]


def flat(x):
    return x.reshape(Q * C, x.shape[-1])


def first_kernel(
    core, dofs_in, star_in, stiffness_in, send_list_in,
    early, later, inner, outer, rows, pick,
    cur, pad, dofs, star, stiffness, send_list, done,
):
    small = [
        pltpu.make_async_copy(stiffness_in, stiffness, done.at[18]),
        pltpu.make_async_copy(send_list_in, send_list, done.at[19]),
    ]
    fields = [pltpu.make_async_copy(dofs_in.at[q], dofs.at[q], done.at[q]) for q in range(Q)]
    stars = [pltpu.make_async_copy(star_in.at[p], star.at[p], done.at[Q + p]) for p in range(Q)]
    for copy in small + fields + stars:
        copy.start()
    for q in range(Q):
        cur[0, q, 32:C, :] = jnp.zeros((8, E), F32)
    small[0].wait()
    small[1].wait()
    rows[...] = stiffness_rows(stiffness, False, -1.0, pad)
    pick[...] = send_pick(core, send_list)
    for q in range(Q):
        fields[q].wait()
        cur[0, q, 0:35, :] = dofs[q]
        early[q] = cur[0, q]
        later[q] = cur[0, q]

    def add(level, p, value):
        k = level + 1
        early[p] = early[p] + value * (1.0 / math.factorial(k + 1))
        later[p] = later[p] + value * ((2.0 ** (k + 1) - 1.0) / math.factorial(k + 1))

    for copy in stars:
        copy.wait()
    taylor(star, rows[...], cur, E, add)
    sent = both(flat(early[...]), pick[...])
    inner[...] = sent[:, :LANES]
    outer[...] = sent[:, LANES:]


def send_pick(core, send_list):
    spread = (iota((32, GHOST), 0) == iota((32, GHOST), 1) % 32).astype(F32)
    table = exact(send_list[...].astype(F32), spread)
    message = iota((8, GHOST), 1) // 32
    row = jnp.where(message < 4, 3 - message, jnp.where(message == 4, 4, 12 - message))
    row = jnp.where(core[0] == 0, row, 7 - row)
    wanted = jnp.sum(jnp.where(row == iota((8, GHOST), 0), table, 0.0), axis=0, keepdims=True)
    wanted = wanted.astype(jnp.int32)
    return jnp.where(iota((E, GHOST), 0) == wanted, 1.0, 0.0).astype(BF16)


def ghost_columns(core, neighbour):
    ghost = neighbour - E
    o = ghost >> 5
    offset = jnp.where(o < 4, o - 4, o - 3)
    offset = jnp.where(core[0] == 0, offset, -offset)
    place = jnp.where(offset > 0, (5 - offset) & 3, 3 - offset)
    return jnp.where(neighbour < E, neighbour, E + place * 32 + (ghost & 31))


def fast_rows(cluster):
    fast = cluster == 0
    before = (iota((E, E), 0) < iota((E, E), 1)).astype(F32).astype(BF16)
    rank = mxu(jnp.where(fast, 1.0, 0.0).astype(BF16), before).astype(jnp.int32)
    return jnp.where((iota((F, E), 0) == rank) & fast, 1.0, 0.0).astype(BF16)


def second_kernel(
    core, dofs, star, minus, plus, cluster, neighbour, codes, early, later, pick,
    stiffness, proj, lift, turn, outer,
    field, star_f, plus_f, lines_f, scatter, nb_all, volume_rows, lift_rows, turn_rows, proj_rows, kept,
    near_medium, steady, route,
    minus_f, early_f, face, flow, near, pad, pad_lift, pad_turn,
):
    kept[...] = outer[...]
    volume_rows[...] = stiffness_rows(stiffness, True, 1.0, pad)
    pad_lift[32:C, :] = jnp.zeros((8, 192), F32)
    total = jnp.zeros((35, 192), F32)
    for i in range(4):
        place = (iota((15, 192), 1) % 64 == i * G + iota((15, 192), 0)).astype(F32)
        total = total - exact(lift[:, i, :], place, (((0,), (0,)), ((), ())))
    pad_lift[0:35, :] = total
    lift_rows[...] = three(pad_lift[...], 128)
    place = (iota((35, 144), 1) % 48 == iota((35, 144), 0)).astype(F32)
    pad_turn[...] = jnp.zeros((192, 144), F32)
    for i in range(4):
        pad_turn[i * G : i * G + 15, :] = exact(proj[:, i, :], place)
    proj_rows[...] = three(pad_turn[0:64, :], 96)
    projs = [exact(proj[:, i, :], place) for i in range(4)]
    for i in range(4):
        for h in range(3):
            at = (3 * i + h) * G
            pad_turn[at : at + 15, :] = exact(turn[h], projs[i])
    turn_rows[...] = three(pad_turn[...], 96)

    kinds = cluster[...]
    picks = fast_rows(kinds)
    scatter[...] = picks
    column = iota((8, E), 1)
    which = jnp.where(iota((8, E), 0) == 0, column // LANES, column % LANES).astype(F32).astype(BF16)
    found = mxu(which, picks, (((1,), (1,)), ((), ()))).astype(jnp.int32)
    block, lane = found[0:1], found[1:2]

    def take(x):
        r = x.shape[0]
        at = jnp.broadcast_to(lane, (r, F))
        got = [lane_gather(x[:, s], at) for s in lanes_of(E)]
        return jnp.where(block == 0, got[0], jnp.where(block == 1, got[1], got[2]))

    for q in range(Q):
        field[q, 32:C, :] = jnp.zeros((8, F), F32)
        field[q, 0:32, :] = take(dofs[q, 0:32, :])
        field[q, 32:35, :] = take(dofs[q, 32:35, :])
        early_f[q] = take(early[q])

    @pl.loop(0, Q)
    def _(p):
        for q in range(Q):
            star_f[p, q] = take(star[p, q])
            minus_f[p, q] = take(minus[p, q])
            plus_f[p, q] = take(plus[p, q])

    table = ghost_columns(core, neighbour[...])
    nb_all[...] = table
    nb = take(table)
    code = take(codes[...])
    lines_f[0:4, :] = nb
    lines_f[4:8, :] = code

    own_faces(early_f, proj_rows[...], face, F)
    flux(minus_f, face, flow, F, False)
    parts = split(flat(early[...]))
    near[...] = gathered([(parts, 0, None)], nb, F)
    near_faces(near, code, turn_rows[...], face, F)
    flux(plus_f, face, flow, F, True)
    near_medium[...] = gathered([(parts, 0, kinds == 1)], table, E)
    steady[...] = both(jnp.where(kinds == 0, 0.0, flat(later[...])), pick[...])
    route[...] = mxu(picks, pick[...]).astype(BF16)

    for p in range(Q):
        field[p] = (
            field[p]
            + halves(mxu(volume_rows[...], star_times(star_f, early_f, p, F)))
            + mxu(lift_rows[...], three_parts(flow[p]))
        )


def third_kernel(
    rows, a, b, q_in, field, star_f, plus_f, lines_f, steady, route, lift_rows, turn_rows,
    moved_f, late_f, inner, outer,
    cur, face, flow, near,
):
    ghosts = split(ghost_array(a, b, q_in))
    near[...] = gathered([(ghosts, E, None)], lines_f[0:4, :], F)
    near_faces(near, lines_f[4:8, :], turn_rows[...], face, F)
    flux(plus_f, face, flow, F, False)
    for p in range(Q):
        value = field[p] + mxu(lift_rows[...], three_parts(flow[p]))
        cur[0, p] = value
        moved_f[p] = value
        late_f[p] = value

    def add(level, p, value):
        late_f[p] = late_f[p] + value * (1.0 / math.factorial(level + 2))

    taylor(star_f, rows[...], cur, F, add)
    sent = steady[...] + both(flat(late_f[...]), route[...])
    inner[...] = sent[:, :LANES]
    outer[...] = sent[:, LANES:]


def spread_kernel(moved_f, late_f, scatter, cluster, later, dofs, start, late):
    fast = cluster[...] == 0
    moved = both(flat(moved_f[...]), scatter[...])
    fresh = both(flat(late_f[...]), scatter[...])
    for p in range(Q):
        rows = slice(p * C, (p + 1) * C)
        late[p] = jnp.where(fast, fresh[rows], later[p])
        start[p] = moved[rows]
        start[p, 0:35, :] = jnp.where(fast, start[p, 0:35, :], dofs[p])


def ghost_array(a, b, q_in):
    part = iota((Q * C, LANES), 1) // 32
    mine = jnp.where((part == 0) | (part == 3), a[...], b[...])
    return jnp.concatenate([mine, q_in[...]], axis=1)


def fourth_kernel(
    start, star, minus, plus, cluster, nb_all, codes, early, late, near_medium,
    a, b, q_in, volume_rows, lift_rows, turn_rows, proj_rows, outer,
    out, kept,
    own, face, flow, near,
):
    kept[...] = outer[...]
    kinds = cluster[...]
    for p in range(Q):
        own[p] = jnp.where(kinds == 0, late[p], early[p] + late[p])
    own_faces(own, proj_rows[...], face, E)
    flux(minus, face, flow, E, False)
    parts = [
        (split(flat(late[...])), 0, None),
        (split(ghost_array(a, b, q_in)), E, kinds == 1),
    ]
    near[...] = gathered(parts, nb_all[...], E, near_medium[...])
    near_faces(near, codes[...], turn_rows[...], face, E)
    flux(plus, face, flow, E, True)
    for p in range(Q):
        out[p] = (
            start[p]
            + halves(mxu(volume_rows[...], star_times(star, own, p, E)))
            + mxu(lift_rows[...], three_parts(flow[p]))
        )


def fifth_kernel(
    dofs, plus, cluster, nb_all, codes, partial, a, b, q_in, lift_rows, turn_rows,
    out, face, flow, near,
):
    ghosts = split(ghost_array(a, b, q_in))
    near[...] = gathered([(ghosts, E, None)], nb_all[...], E)
    near_faces(near, codes[...], turn_rows[...], face, E)
    flux(plus, face, flow, E, False)
    active = cluster[...] < 2
    for p in range(Q):
        value = partial[p] + mxu(lift_rows[...], three_parts(flow[p]))
        out[p] = jnp.where(active, value[0:35], dofs[p])


def call(kernel, outs, args, scratch, scalars=0, copies=0, micros=5):
    vmem = pl.BlockSpec(memory_space=pltpu.VMEM)
    smem = pl.BlockSpec(memory_space=pltpu.SMEM)
    place = pl.BlockSpec(memory_space=pl.ANY) if copies else vmem
    if copies:
        args = args[:scalars] + [
            pltpu.with_memory_space_constraint(x, pltpu.HBM) for x in args[scalars:]
        ]
    return pl.pallas_call(
        kernel,
        out_shape=[jax.ShapeDtypeStruct(*o) for o in outs],
        in_specs=[smem] * scalars + [place] * (len(args) - scalars),
        out_specs=[vmem] * len(outs),
        scratch_shapes=[pltpu.VMEM(*s) for s in scratch]
        + ([pltpu.SemaphoreType.DMA((copies,))] if copies else []),
        compiler_params=pltpu.CompilerParams(vmem_limit_bytes=10 * 1024 * 1024),
        cost_estimate=pl.CostEstimate(
            flops=int(micros * 1e9), bytes_accessed=1 << 20, transcendentals=0
        ),
        name=kernel.__name__,
    )(*args)


def to_chips(inner, outer):
    count = lax.axis_size("dom")
    chips = count // 2

    def along(reach):
        def target(device):
            chip, core = device // 2, device % 2
            to = chip + (reach if core == 0 else -reach)
            return 2 * to + core if 0 <= to < chips else device ^ 1

        return [(device, target(device)) for device in range(count)]

    beside = to_pair(inner)
    first = iota((1, LANES), 1) < 64
    a = lax.ppermute(jnp.where(first, beside, outer), "dom", along(1))
    b = lax.ppermute(jnp.where(first, outer, beside), "dom", along(2))
    return a, b


def to_pair(value):
    count = lax.axis_size("dom")
    return lax.ppermute(value, "dom", [(device, device ^ 1) for device in range(count)])


def handed_on(outer, a, b):
    part = iota((1, LANES), 1) // 32
    return jnp.where(part == 0, outer, jnp.where(part == 3, b, a))


def body(
    dofs,
    star,
    flux_minus,
    flux_plus,
    cluster,
    neighbour,
    face_code,
    send_list,
    stiffness,
    face_proj,
    face_lift,
    face_turn,
):
    core = (lax.axis_index("dom") % 2).astype(jnp.int32).reshape(1)
    cluster = cluster.reshape(1, E)
    star, flux_minus, flux_plus = (
        jnp.transpose(x, (1, 2, 0, 3)) for x in (star, flux_minus, flux_plus)
    )
    face_proj, face_lift = jnp.transpose(face_proj, (1, 0, 2)), jnp.transpose(face_lift, (2, 0, 1))
    whole, compact, block = (Q, C, E), (Q, C, F), (Q * C, LANES)
    early, later, inner, outer, rows, pick = call(
        first_kernel,
        [
            (whole, F32), (whole, F32), (block, F32), (block, F32),
            ((2 * C, 256), BF16), ((E, GHOST), BF16),
        ],
        [core, dofs, star, stiffness, send_list],
        [
            ((2,) + whole, F32), ((C, 256), F32), ((Q, 35, E), F32), ((Q, Q, 3, E), F32),
            ((3, 35, 35), F32), ((8, 32), jnp.int32),
        ],
        1,
        20,
    )
    a, b = to_chips(inner, outer)
    (
        field, star_f, plus_f, lines_f, scatter, nb_all, volume_rows, lift_rows, turn_rows, proj_rows,
        kept, near_medium, steady, route,
    ) = call(
        second_kernel,
        [
            (compact, F32), ((Q, Q, 3, F), F32), ((Q, Q, 4, F), F32), ((8, F), jnp.int32),
            ((F, E), BF16), ((4, E), jnp.int32),
            ((2 * C, 256), BF16), ((C, 192), BF16), ((192, 144), BF16), ((64, 144), BF16),
            (block, F32), ((Q * C, 4 * E), F32), ((Q * C, GHOST), F32), ((F, GHOST), BF16),
        ],
        [
            core, dofs, star, flux_minus, flux_plus, cluster, neighbour, face_code, early, later, pick,
            stiffness, face_proj, face_lift, face_turn, outer,
        ],
        [
            ((Q, Q, 4, F), F32), (compact, F32), ((Q, 64, F), F32), ((Q, 64, F), F32),
            ((Q * C, 4 * F), F32), ((C, 256), F32), ((C, 192), F32), ((192, 144), F32),
        ],
        1,
    )
    q_in = to_pair(handed_on(kept, a, b))
    moved_f, late_f, inner, outer = call(
        third_kernel,
        [(compact, F32), (compact, F32), (block, F32), (block, F32)],
        [
            rows, a, b, q_in, field, star_f, plus_f, lines_f, steady, route, lift_rows, turn_rows
        ],
        [
            ((2,) + compact, F32), ((Q, 64, F), F32), ((Q, 64, F), F32), ((Q * C, 4 * F), F32),
        ],
    )
    a2, b2 = to_chips(inner, outer)
    start, late = call(
        spread_kernel,
        [(whole, F32), (whole, F32)],
        [moved_f, late_f, scatter, cluster, later, dofs],
        [],
        micros=1,
    )
    partial, kept = call(
        fourth_kernel,
        [(whole, F32), (block, F32)],
        [
            start, star, flux_minus, flux_plus, cluster, nb_all, face_code, early, late, near_medium,
            a, b, q_in, volume_rows, lift_rows, turn_rows, proj_rows, outer,
        ],
        [(whole, F32), ((Q, 64, E), F32), ((Q, 64, E), F32), ((Q * C, 4 * E), F32)],
    )
    q2 = to_pair(handed_on(kept, a2, b2))
    (out,) = call(
        fifth_kernel,
        [((Q, 35, E), F32)],
        [dofs, flux_plus, cluster, nb_all, face_code, partial, a2, b2, q2, lift_rows, turn_rows],
        [((Q, 64, E), F32), ((Q, 64, E), F32), ((Q * C, 4 * E), F32)],
    )
    return out


def solution(mesh):
    return jax.shard_map(
        body,
        mesh=mesh,
        in_specs=(
            P(None, None, "dom"),
            P(None, None, None, "dom"),
            P(None, None, None, "dom"),
            P(None, None, None, "dom"),
            P("dom"),
            P(None, "dom"),
            P(None, "dom"),
            P(None, "dom"),
            P(),
            P(),
            P(),
            P(),
        ),
        out_specs=P(None, None, "dom"),
        check_vma=False,
    )
```

```python
import functools
import math

import jax
import jax.numpy as jnp
from jax import lax
from jax.experimental import pallas as pl
from jax.experimental.pallas import tpu as pltpu
from jax.sharding import PartitionSpec as P

ORDER = 5
E = 384
F = 128
Q = 9
C = 40
G = 16
GHOST = 256
LANES = 128

HIGH = lax.Precision.HIGHEST
F32 = jnp.float32
BF16 = jnp.bfloat16


def iota(shape, dim):
    return lax.broadcasted_iota(jnp.int32, shape, dim)


def exact(a, b, dims=(((1,), (0,)), ((), ()))):
    return lax.dot_general(a, b, dims, precision=HIGH, preferred_element_type=F32)


def mxu(a, b, dims=(((1,), (0,)), ((), ()))):
    return lax.dot_general(a, b, dims, preferred_element_type=F32)


def split(x):
    high = x.astype(BF16)
    return high, (x - high.astype(F32)).astype(BF16)


def lane_gather(x, at):
    numbers = lax.GatherDimensionNumbers(
        offset_dims=(),
        collapsed_slice_dims=(1,),
        start_index_map=(1,),
        operand_batching_dims=(0,),
        start_indices_batching_dims=(0,),
    )
    mode = lax.GatherScatterMode.PROMISE_IN_BOUNDS
    return lax.gather(x, at[..., None], numbers, (1, 1), mode=mode)


def both(x, right):
    high, low = split(x)
    return mxu(high, right) + mxu(low, right)


def lanes_of(width):
    return [slice(at, at + LANES) for at in range(0, width, LANES)]


def stiffness_rows(stiffness, transposed, sign, pad_ref):
    total = jnp.zeros((35, 256), F32)
    for d in range(3):
        place = (iota((35, 256), 1) % 128 == d * C + iota((35, 256), 0)).astype(F32)
        dims = (((0,), (0,)), ((), ())) if transposed else (((1,), (0,)), ((), ()))
        total = total + exact(stiffness[d], place, dims)
    pad_ref[32:C, :] = jnp.zeros((8, 256), F32)
    pad_ref[0:35, :] = total * sign
    padded = pad_ref[...]
    high, low = split(padded)
    low = jnp.where(iota((C, 256), 1) < 128, low.astype(F32), 0.0)
    return jnp.concatenate([high.astype(F32), low], axis=0).astype(BF16)


def three(rows, first):
    high, low = split(rows)
    keep = iota(rows.shape, 1) < first
    return jnp.where(keep, high.astype(F32), low.astype(F32)).astype(BF16)


def three_parts(x):
    high, low = split(x)
    return jnp.concatenate([high, low, high], axis=0)


def padded48(x):
    return jnp.concatenate([x, jnp.zeros((8, x.shape[1]), F32)], axis=0)


def star_times(star_ref, source, width, p):
    columns = []
    for at in lanes_of(width):
        values = [source[q, :, at] for q in range(Q)]
        parts = []
        for d in range(3):
            total = star_ref[p, 0, d : d + 1, at] * values[0]
            for q in range(1, Q):
                total = total + star_ref[p, q, d : d + 1, at] * values[q]
            parts.append(total)
        parts.append(jnp.zeros((8, LANES), F32))
        high, low = split(jnp.concatenate(parts, axis=0))
        columns.append(jnp.concatenate([high, low], axis=0))
    return jnp.concatenate(columns, axis=1) if len(columns) > 1 else columns[0]


def halves(out):
    return out[:C] + out[C:]


PAIRS = ((0, 1), (2, 3), (4, 5), (6, 7), (8,))


def in_pairs(left, right_of, width):
    for group in PAIRS:
        right = [right_of(p) for p in group]
        out = mxu(left, jnp.concatenate(right, axis=1) if len(right) > 1 else right[0])
        for at, p in enumerate(group):
            yield p, out[:, at * width : (at + 1) * width]


def taylor(star_ref, rows, cur_ref, width, add):
    for level in range(ORDER - 1):
        source, target = cur_ref.at[level % 2], cur_ref.at[(level + 1) % 2]
        right_of = functools.partial(star_times, star_ref, source, width)
        for p, out in in_pairs(rows, right_of, width):
            value = halves(out)
            target[p] = value
            add(level, p, value)


def flux(coefficients, source, target, width, accumulate):
    for i in range(4):
        rows = slice(i * G, (i + 1) * G)
        for at in lanes_of(width):
            values = [source[q, rows, at] for q in range(Q)]
            for p in range(Q):
                total = coefficients[p, 0, i : i + 1, at] * values[0]
                for q in range(1, Q):
                    total = total + coefficients[p, q, i : i + 1, at] * values[q]
                if accumulate:
                    total = target[p, rows, at] + total
                target[p, rows, at] = total


def lifted(lift_rows, flow, width):
    return in_pairs(lift_rows, lambda p: three_parts(flow[p]), width)


def advance(out_ref, start, star_ref, own, flow, volume_rows, lift_rows, width):
    right_of = functools.partial(star_times, star_ref, own, width)
    volume = in_pairs(volume_rows, right_of, width)
    for (p, inside), (_, faces) in zip(volume, lifted(lift_rows, flow, width)):
        out_ref[p] = start[p] + halves(inside) + faces


def own_faces(own, proj_rows, face_ref, width):
    for q, out in in_pairs(proj_rows, lambda q: three_parts(padded48(own[q])), width):
        face_ref[q] = out


def beside(rows):
    return jnp.concatenate([rows[i : i + 1, :] for i in range(4)], axis=1)


def gathered(parts, neighbour, width, total=None):
    wanted = beside(neighbour)
    for arrays, first, mask in parts:
        columns = arrays[0].shape[1]
        hit = iota((columns, 4 * width), 0) + first == wanted
        if mask is not None:
            hit = hit & jnp.concatenate([mask] * 4, axis=1)
        pick = jnp.where(hit, 1.0, 0.0).astype(BF16)
        for array in arrays:
            piece = mxu(array, pick)
            total = piece if total is None else total + piece
    return total


def ghost_pick(neighbour, width):
    hit = iota((GHOST, 4 * width), 0) + E == beside(neighbour)
    return jnp.where(hit, 1.0, 0.0).astype(BF16)


def near_parts(near_refs, q):
    values = [padded48(ref[q * C : (q + 1) * C, :]) for ref in near_refs]
    if len(values) == 1:
        return three_parts(values[0])
    high, low = [value.astype(BF16) for value in values]
    return jnp.concatenate([high, low, high], axis=0)


def near_faces(near_refs, codes, turn_rows, face_ref, width):
    code = beside(codes)
    for q in range(Q):
        every = mxu(turn_rows, near_parts(near_refs, q))
        chosen = every[0:G]
        for k in range(1, 12):
            chosen = jnp.where(code == k, every[k * G : (k + 1) * G], chosen)
        for i in range(4):
            face_ref[q, i * G : (i + 1) * G, :] = chosen[:, i * width : (i + 1) * width]


def flat(x):
    return x.reshape(Q * C, x.shape[-1])


def first_kernel(
    core, dofs_in, star_in, stiffness_in, send_list_in,
    early, later, inner, outer, rows, pick,
    cur, pad, dofs, star, stiffness, send_list, done,
):
    small = [
        pltpu.make_async_copy(stiffness_in, stiffness, done.at[18]),
        pltpu.make_async_copy(send_list_in, send_list, done.at[19]),
    ]
    fields = [pltpu.make_async_copy(dofs_in.at[q], dofs.at[q], done.at[q]) for q in range(Q)]
    stars = [pltpu.make_async_copy(star_in.at[p], star.at[p], done.at[Q + p]) for p in range(Q)]
    for copy in small + fields + stars:
        copy.start()
    for q in range(Q):
        cur[0, q, 32:C, :] = jnp.zeros((8, E), F32)
    small[0].wait()
    small[1].wait()
    rows[...] = stiffness_rows(stiffness, False, -1.0, pad)
    pick[...] = send_pick(core, send_list)
    for q in range(Q):
        fields[q].wait()
        cur[0, q, 0:35, :] = dofs[q]
        early[q] = cur[0, q]
        later[q] = cur[0, q]

    def add(level, p, value):
        k = level + 1
        early[p] = early[p] + value * (1.0 / math.factorial(k + 1))
        later[p] = later[p] + value * ((2.0 ** (k + 1) - 1.0) / math.factorial(k + 1))

    for copy in stars:
        copy.wait()
    taylor(star, rows[...], cur, E, add)
    sent = both(flat(early[...]), pick[...])
    inner[...] = sent[:, :LANES]
    outer[...] = sent[:, LANES:]


def send_pick(core, send_list):
    spread = (iota((32, GHOST), 0) == iota((32, GHOST), 1) % 32).astype(F32)
    table = exact(send_list[...].astype(F32), spread)
    message = iota((8, GHOST), 1) // 32
    row = jnp.where(message < 4, 3 - message, jnp.where(message == 4, 4, 12 - message))
    row = jnp.where(core[0] == 0, row, 7 - row)
    wanted = jnp.sum(jnp.where(row == iota((8, GHOST), 0), table, 0.0), axis=0, keepdims=True)
    wanted = wanted.astype(jnp.int32)
    return jnp.where(iota((E, GHOST), 0) == wanted, 1.0, 0.0).astype(BF16)


def ghost_columns(core, neighbour):
    ghost = neighbour - E
    o = ghost >> 5
    offset = jnp.where(o < 4, o - 4, o - 3)
    offset = jnp.where(core[0] == 0, offset, -offset)
    place = jnp.where(offset > 0, (5 - offset) & 3, 3 - offset)
    return jnp.where(neighbour < E, neighbour, E + place * 32 + (ghost & 31))


def fast_rows(cluster):
    fast = cluster == 0
    before = (iota((E, E), 0) < iota((E, E), 1)).astype(F32).astype(BF16)
    rank = mxu(jnp.where(fast, 1.0, 0.0).astype(BF16), before).astype(jnp.int32)
    return jnp.where((iota((F, E), 0) == rank) & fast, 1.0, 0.0).astype(BF16)


def second_kernel(
    core, dofs, star, minus, plus, cluster, neighbour, codes, early, later, pick,
    stiffness, proj, lift, turn, outer,
    field, star_f, plus_f, lines_f, scatter, nb_all, volume_rows, lift_rows, turn_rows, proj_rows, kept,
    near_medium, steady, route,
    minus_f, early_f, face, flow, near, pad, pad_lift, pad_turn,
):
    kept[...] = outer[...]
    volume_rows[...] = stiffness_rows(stiffness, True, 1.0, pad)
    pad_lift[32:C, :] = jnp.zeros((8, 192), F32)
    total = jnp.zeros((35, 192), F32)
    for i in range(4):
        place = (iota((15, 192), 1) % 64 == i * G + iota((15, 192), 0)).astype(F32)
        total = total - exact(lift[:, i, :], place, (((0,), (0,)), ((), ())))
    pad_lift[0:35, :] = total
    lift_rows[...] = three(pad_lift[...], 128)
    place = (iota((35, 144), 1) % 48 == iota((35, 144), 0)).astype(F32)
    pad_turn[...] = jnp.zeros((192, 144), F32)
    for i in range(4):
        pad_turn[i * G : i * G + 15, :] = exact(proj[:, i, :], place)
    proj_rows[...] = three(pad_turn[0:64, :], 96)
    projs = [exact(proj[:, i, :], place) for i in range(4)]
    for i in range(4):
        for h in range(3):
            at = (3 * i + h) * G
            pad_turn[at : at + 15, :] = exact(turn[h], projs[i])
    turn_rows[...] = three(pad_turn[...], 96)

    kinds = cluster[...]
    picks = fast_rows(kinds)
    scatter[...] = picks
    column = iota((8, E), 1)
    which = jnp.where(iota((8, E), 0) == 0, column // LANES, column % LANES).astype(F32).astype(BF16)
    found = mxu(which, picks, (((1,), (1,)), ((), ()))).astype(jnp.int32)
    block, lane = found[0:1], found[1:2]

    def take(x):
        r = x.shape[0]
        at = jnp.broadcast_to(lane, (r, F))
        got = [lane_gather(x[:, s], at) for s in lanes_of(E)]
        return jnp.where(block == 0, got[0], jnp.where(block == 1, got[1], got[2]))

    for q in range(Q):
        field[q, 32:C, :] = jnp.zeros((8, F), F32)
        field[q, 0:32, :] = take(dofs[q, 0:32, :])
        field[q, 32:35, :] = take(dofs[q, 32:35, :])
        early_f[q] = take(early[q])

    @pl.loop(0, Q)
    def _(p):
        for q in range(Q):
            star_f[p, q] = take(star[p, q])
            minus_f[p, q] = take(minus[p, q])
            plus_f[p, q] = take(plus[p, q])

    table = ghost_columns(core, neighbour[...])
    nb_all[...] = table
    nb = take(table)
    code = take(codes[...])
    lines_f[0:4, :] = nb
    lines_f[4:8, :] = code

    own_faces(early_f, proj_rows[...], face, F)
    flux(minus_f, face, flow, F, False)
    parts = split(flat(early[...]))
    near[...] = gathered([(parts, 0, None)], nb, F)
    near_faces([near], code, turn_rows[...], face, F)
    flux(plus_f, face, flow, F, True)
    near_medium[...] = gathered([(parts, 0, kinds == 1)], table, E)
    steady[...] = both(jnp.where(kinds == 0, 0.0, flat(later[...])), pick[...])
    route[...] = mxu(picks, pick[...]).astype(BF16)

    advance(field, field, star_f, early_f, flow, volume_rows[...], lift_rows[...], F)


def third_kernel(
    rows, a, b, q_in, field, star_f, plus_f, lines_f, steady, route, lift_rows, turn_rows,
    moved_f, late_f, inner, outer,
    cur, face, flow, near,
):
    columns = ghost_pick(lines_f[0:4, :], F)
    for at, part in enumerate(split(ghost_array(a, b, q_in))):
        near[at] = mxu(part, columns)
    near_faces([near.at[0], near.at[1]], lines_f[4:8, :], turn_rows[...], face, F)
    flux(plus_f, face, flow, F, False)
    for p, faces in lifted(lift_rows[...], flow, F):
        value = field[p] + faces
        cur[0, p] = value
        moved_f[p] = value
        late_f[p] = value

    def add(level, p, value):
        late_f[p] = late_f[p] + value * (1.0 / math.factorial(level + 2))

    taylor(star_f, rows[...], cur, F, add)
    sent = steady[...] + both(flat(late_f[...]), route[...])
    inner[...] = sent[:, :LANES]
    outer[...] = sent[:, LANES:]


def spread_kernel(moved_f, late_f, scatter, cluster, later, dofs, nb_all, start, late, columns):
    columns[...] = ghost_pick(nb_all[...], E)
    fast = cluster[...] == 0
    moved = both(flat(moved_f[...]), scatter[...])
    fresh = both(flat(late_f[...]), scatter[...])
    for p in range(Q):
        rows = slice(p * C, (p + 1) * C)
        late[p] = jnp.where(fast, fresh[rows], later[p])
        start[p] = moved[rows]
        start[p, 0:35, :] = jnp.where(fast, start[p, 0:35, :], dofs[p])


def ghost_array(a, b, q_in):
    part = iota((Q * C, LANES), 1) // 32
    mine = jnp.where((part == 0) | (part == 3), a[...], b[...])
    return jnp.concatenate([mine, q_in[...]], axis=1)


def fourth_kernel(
    start, star, minus, plus, cluster, nb_all, codes, early, late, near_medium,
    a, b, q_in, volume_rows, lift_rows, turn_rows, proj_rows, outer,
    out, kept,
    own, face, flow, near,
):
    kept[...] = outer[...]
    kinds = cluster[...]
    for p in range(Q):
        own[p] = jnp.where(kinds == 0, late[p], early[p] + late[p])
    own_faces(own, proj_rows[...], face, E)
    flux(minus, face, flow, E, False)
    parts = [
        (split(flat(late[...])), 0, None),
        (split(ghost_array(a, b, q_in)), E, kinds == 1),
    ]
    near[...] = gathered(parts, nb_all[...], E, near_medium[...])
    near_faces([near], codes[...], turn_rows[...], face, E)
    flux(plus, face, flow, E, True)
    advance(out, start, star, own, flow, volume_rows[...], lift_rows[...], E)


def fifth_kernel(
    dofs, plus, cluster, columns, codes, partial, a, b, q_in, lift_rows, turn_rows,
    out, face, flow, near,
):
    for at, part in enumerate(split(ghost_array(a, b, q_in))):
        near[at] = mxu(part, columns[...])
    near_faces([near.at[0], near.at[1]], codes[...], turn_rows[...], face, E)
    flux(plus, face, flow, E, False)
    active = cluster[...] < 2
    for p, faces in lifted(lift_rows[...], flow, E):
        value = partial[p] + faces
        out[p] = jnp.where(active, value[0:35], dofs[p])


def call(kernel, outs, args, scratch, scalars=0, copies=0, micros=5):
    vmem = pl.BlockSpec(memory_space=pltpu.VMEM)
    smem = pl.BlockSpec(memory_space=pltpu.SMEM)
    place = pl.BlockSpec(memory_space=pl.ANY) if copies else vmem
    if copies:
        args = args[:scalars] + [
            pltpu.with_memory_space_constraint(x, pltpu.HBM) for x in args[scalars:]
        ]
    return pl.pallas_call(
        kernel,
        out_shape=[jax.ShapeDtypeStruct(*o) for o in outs],
        in_specs=[smem] * scalars + [place] * (len(args) - scalars),
        out_specs=[vmem] * len(outs),
        scratch_shapes=[pltpu.VMEM(*s) for s in scratch]
        + ([pltpu.SemaphoreType.DMA((copies,))] if copies else []),
        compiler_params=pltpu.CompilerParams(vmem_limit_bytes=10 * 1024 * 1024),
        cost_estimate=pl.CostEstimate(
            flops=int(micros * 1e9), bytes_accessed=1 << 20, transcendentals=0
        ),
        name=kernel.__name__,
    )(*args)


def to_chips(inner, outer):
    count = lax.axis_size("dom")
    chips = count // 2

    def along(reach):
        def target(device):
            chip, core = device // 2, device % 2
            to = chip + (reach if core == 0 else -reach)
            return 2 * to + core if 0 <= to < chips else device ^ 1

        return [(device, target(device)) for device in range(count)]

    beside = to_pair(inner)
    first = iota((1, LANES), 1) < 64
    a = lax.ppermute(jnp.where(first, beside, outer), "dom", along(1))
    b = lax.ppermute(jnp.where(first, outer, beside), "dom", along(2))
    return a, b


def to_pair(value):
    count = lax.axis_size("dom")
    return lax.ppermute(value, "dom", [(device, device ^ 1) for device in range(count)])


def handed_on(outer, a, b):
    part = iota((1, LANES), 1) // 32
    return jnp.where(part == 0, outer, jnp.where(part == 3, b, a))


def body(
    dofs,
    star,
    flux_minus,
    flux_plus,
    cluster,
    neighbour,
    face_code,
    send_list,
    stiffness,
    face_proj,
    face_lift,
    face_turn,
):
    core = (lax.axis_index("dom") % 2).astype(jnp.int32).reshape(1)
    cluster = cluster.reshape(1, E)
    star, flux_minus, flux_plus = (
        jnp.transpose(x, (1, 2, 0, 3)) for x in (star, flux_minus, flux_plus)
    )
    face_proj, face_lift = jnp.transpose(face_proj, (1, 0, 2)), jnp.transpose(face_lift, (2, 0, 1))
    whole, compact, block = (Q, C, E), (Q, C, F), (Q * C, LANES)
    early, later, inner, outer, rows, pick = call(
        first_kernel,
        [
            (whole, F32), (whole, F32), (block, F32), (block, F32),
            ((2 * C, 256), BF16), ((E, GHOST), BF16),
        ],
        [core, dofs, star, stiffness, send_list],
        [
            ((2,) + whole, F32), ((C, 256), F32), ((Q, 35, E), F32), ((Q, Q, 3, E), F32),
            ((3, 35, 35), F32), ((8, 32), jnp.int32),
        ],
        1,
        20,
    )
    a, b = to_chips(inner, outer)
    (
        field, star_f, plus_f, lines_f, scatter, nb_all, volume_rows, lift_rows, turn_rows, proj_rows,
        kept, near_medium, steady, route,
    ) = call(
        second_kernel,
        [
            (compact, F32), ((Q, Q, 3, F), F32), ((Q, Q, 4, F), F32), ((8, F), jnp.int32),
            ((F, E), BF16), ((4, E), jnp.int32),
            ((2 * C, 256), BF16), ((C, 192), BF16), ((192, 144), BF16), ((64, 144), BF16),
            (block, F32), ((Q * C, 4 * E), F32), ((Q * C, GHOST), F32), ((F, GHOST), BF16),
        ],
        [
            core, dofs, star, flux_minus, flux_plus, cluster, neighbour, face_code, early, later, pick,
            stiffness, face_proj, face_lift, face_turn, outer,
        ],
        [
            ((Q, Q, 4, F), F32), (compact, F32), ((Q, 64, F), F32), ((Q, 64, F), F32),
            ((Q * C, 4 * F), F32), ((C, 256), F32), ((C, 192), F32), ((192, 144), F32),
        ],
        1,
    )
    q_in = to_pair(handed_on(kept, a, b))
    moved_f, late_f, inner, outer = call(
        third_kernel,
        [(compact, F32), (compact, F32), (block, F32), (block, F32)],
        [
            rows, a, b, q_in, field, star_f, plus_f, lines_f, steady, route, lift_rows, turn_rows
        ],
        [
            ((2,) + compact, F32), ((Q, 64, F), F32), ((Q, 64, F), F32), ((2, Q * C, 4 * F), F32),
        ],
    )
    a2, b2 = to_chips(inner, outer)
    start, late, columns = call(
        spread_kernel,
        [(whole, F32), (whole, F32), ((GHOST, 4 * E), BF16)],
        [moved_f, late_f, scatter, cluster, later, dofs, nb_all],
        [],
        micros=1,
    )
    partial, kept = call(
        fourth_kernel,
        [(whole, F32), (block, F32)],
        [
            start, star, flux_minus, flux_plus, cluster, nb_all, face_code, early, late, near_medium,
            a, b, q_in, volume_rows, lift_rows, turn_rows, proj_rows, outer,
        ],
        [(whole, F32), ((Q, 64, E), F32), ((Q, 64, E), F32), ((Q * C, 4 * E), F32)],
    )
    q2 = to_pair(handed_on(kept, a2, b2))
    (out,) = call(
        fifth_kernel,
        [((Q, 35, E), F32)],
        [dofs, flux_plus, cluster, columns, face_code, partial, a2, b2, q2, lift_rows, turn_rows],
        [((Q, 64, E), F32), ((Q, 64, E), F32), ((2, Q * C, 4 * E), F32)],
    )
    return out


def solution(mesh):
    return jax.shard_map(
        body,
        mesh=mesh,
        in_specs=(
            P(None, None, "dom"),
            P(None, None, None, "dom"),
            P(None, None, None, "dom"),
            P(None, None, None, "dom"),
            P("dom"),
            P(None, "dom"),
            P(None, "dom"),
            P(None, "dom"),
            P(),
            P(),
            P(),
            P(),
        ),
        out_specs=P(None, None, "dom"),
        check_vma=False,
    )
```
